32 devices in a mesh: occ: 4 (over y, x), vir: 8 (over z, core).
Axes of the slice: x: 2, y: 2, z: 4, core: 2. Of those that a mesh axis runs over, the one named last changes fastest.
Arguments:
- amplitudes: float32 [4, 1024, 1024], P(None, 'occ', 'vir'), may hold values from -6 to 6
- integrals: float32 [4, 7168, 1024], P(None, 'vir', 'occ'), may hold values from -0.1875 to 0.1875
Outputs:
- ladder: float32 [4, 1024, 7168], P(None, 'occ', 'vir')
The draws below stay inside these ranges and needn't reach their ends.
All inputs are finite; a program needn't handle non-finite values.
Results may differ from the reference program's by a relative error of at most 0.000073.
Values sent between devices are 32-bit elements; how exact they have to be, the bound alone decides.
No kernel may reach another device: no remote copies, remote signals or barrier semaphores. Data moves between devices by JAX's collectives and lax.ppermute only.
A program may use at most 64 MiB of HBM per device.

```python
import jax
import jax.numpy as jnp
from jax import lax

NIRREP = 4
IJ_G = 1024
CD_G = 1024
AB_G = 7168


def shard_levels(key, dims, cuts, low, largest):
    def one(dim, shards_of):
        steps = jax.random.uniform(jax.random.fold_in(jax.random.fold_in(key, 6), dim), (shards_of,), jnp.float32, low / len(cuts), largest / len(cuts))
        return jnp.repeat(jnp.exp(steps), dims[dim] // shards_of).reshape((-1,) + (1,) * (len(dims) - dim - 1))

    gain = one(*cuts[0])
    for cut in cuts[1:]:
        gain = gain * one(*cut)
    return gain


def bell_draw(stream_key, shape, width, bound, split=(), kind=jnp.bfloat16):
    result = jax.random.normal(stream_key, shape, jnp.float32) * width
    if len(split) > 0:
        result = shard_levels(stream_key, shape, split, -0.22, 0.18) * result
    return jnp.clip(result, min=-bound, max=bound).astype(kind)


def setup_inputs(seed: int = 0) -> dict:
    streams_of = jax.random.split(jax.random.key(seed), 3)
    amplitudes = bell_draw(streams_of[0], (NIRREP, IJ_G, CD_G), 1.0, 6.0, ((1, 4), (2, 8)), jnp.float32)
    integrals = bell_draw(streams_of[1], (NIRREP, AB_G, CD_G), CD_G ** -0.5, 0.1875, ((1, 8), (2, 4)), jnp.float32)
    return {"amplitudes": amplitudes, "integrals": integrals}


def reference(amplitudes, integrals):
    panel_sum = lax.dot_general(amplitudes, integrals, (((2,), (2,)), ((0,), (0,))), precision=lax.Precision.HIGHEST, preferred_element_type=jnp.float32)
    return 0.5 * panel_sum
```

```python
import functools

import jax
import jax.numpy as jnp
from jax import lax
from jax.experimental import pallas as pl
from jax.experimental.pallas import tpu as pltpu
from jax.sharding import PartitionSpec as P

MESH = {"occ": 4, "vir": 8}


def contract_block(left, piece):
    return lax.dot_general(
        left,
        piece,
        (((2,), (2,)), ((0,), (0,))),
        precision=lax.Precision.HIGHEST,
        preferred_element_type=jnp.float32,
    )


def gather_body(amplitudes, integrals):
    gathered = lax.all_gather(amplitudes, "vir", axis=2, tiled=True)
    panel_sum = contract_block(gathered, lax.all_gather(integrals, "occ", axis=2, tiled=True))
    return 0.5 * panel_sum


BOTH = ("occ", "vir")
OVER = ([(o, o ^ 1) for o in range(4)], [(o, o ^ 2) for o in range(4)])
OVER_CORE = [(v, v ^ 1) for v in range(8)]


def pairs(move):
    return [(o * 8 + v, move(o, v >> 1, v & 1)) for o in range(4) for v in range(8)]


SAME_CORE = pairs(lambda o, z, c: (o ^ (1 if c else 2)) * 8 + 2 * z + c)
CROSS_CORE = pairs(lambda o, z, c: (o ^ (2 if c else 1)) * 8 + 2 * z + 1 - c)
FIRST_Z = pairs(lambda o, z, c: o * 8 + 2 * (z ^ (1 if c else 2)) + c)
SECOND_Z = pairs(lambda o, z, c: o * 8 + 2 * (z ^ (2 if c else 1)) + c)


def split(a):
    high = a.astype(jnp.bfloat16)
    low = (a - high.astype(jnp.float32)).astype(jnp.bfloat16)
    return high, low


def dot3(left, right):
    (lh, ll), (rh, rl) = left, right

    def dot(a, b):
        return lax.dot_general(a, b, (((1,), (1,)), ((), ())), preferred_element_type=jnp.float32)

    return dot(lh, rh) + (dot(lh, rl) + dot(ll, rh))


def partial_kernel(kind, i, place, same0, same1, other0, other1, own_ref, got_ref, out_ref):
    y, x, z, core = place[0], place[1], place[2], place[3]
    first_half, own_half = (lax.rem(z, 2), x) if kind == 0 else (z // 2, y)
    in_order = first_half == own_half

    def rows(a, b):
        return jnp.concatenate([jnp.where(core == kind, a[c, i], b[c, i]) for c in range(2)], axis=1)

    first, second = rows(same0, other0), rows(same1, other1)
    t = split(jnp.concatenate([jnp.where(in_order, first, second), jnp.where(in_order, second, first)], axis=1))
    width = own_ref.shape[0]
    step = 256
    for start in range(0, width, step):
        size = min(step, width - start)
        v = split(jnp.concatenate([own_ref[start : start + size, :], got_ref[start : start + size, :]], axis=1))
        out_ref[:, start : start + size] = dot3(t, v)


def partial_sum(kind, i, place, blocks, own, got):
    n_ij, n_ab, n_cd = blocks[0].shape[2], own.shape[0], 2 * own.shape[1]
    vmem = pl.BlockSpec(memory_space=pltpu.VMEM)
    return pl.pallas_call(
        functools.partial(partial_kernel, kind, i),
        out_shape=jax.ShapeDtypeStruct((n_ij, n_ab), jnp.float32),
        in_specs=[pl.BlockSpec(memory_space=pltpu.SMEM)] + [vmem] * 6,
        out_specs=vmem,
        compiler_params=pltpu.CompilerParams(vmem_limit_bytes=32 * 1024 * 1024),
        cost_estimate=pl.CostEstimate(
            flops=6 * n_ij * n_ab * n_cd, bytes_accessed=4 * (2 * n_ij * n_cd + n_ab * n_cd + n_ij * n_ab), transcendentals=0
        ),
    )(place, *blocks, own, got)


def spread(first, second, core, holder):
    first, second = jnp.where(core == 0, first, second), jnp.where(core == 0, second, first)
    held = jnp.stack([first, second])
    near = jnp.where(holder, held, lax.ppermute(held, BOTH, FIRST_Z))
    far = lax.ppermute(near, BOTH, SECOND_Z)
    return near, far, lax.ppermute(near, "vir", OVER_CORE), lax.ppermute(far, "vir", OVER_CORE)


def hybrid_body(amplitudes, integrals):
    o, v = lax.axis_index("occ"), lax.axis_index("vir")
    y, x, z, core = o // 2, o % 2, v // 2, v % 2
    place = jnp.stack([y, x, z, core]).astype(jnp.int32)
    holder = jnp.where(core == 0, z // 2 == y, z % 2 == x)
    mine = jnp.where(core == 0, amplitudes[:2], amplitudes[2:])
    give = jnp.where(core == 0, amplitudes[2:], amplitudes[:2])
    same, cross = lax.ppermute(mine, BOTH, SAME_CORE), lax.ppermute(give, BOTH, CROSS_CORE)
    got = {(k, i): lax.ppermute(integrals[2 * k + i], "occ", OVER[k]) for i in range(2) for k in range(2)}
    send_t = spread(same, cross, core, holder)
    keep_t = spread(mine, lax.ppermute(give, "vir", OVER_CORE), core, holder)
    came = {}
    for i in range(2):
        for k in range(2):
            part = partial_sum(k, i, place, send_t, integrals[2 * k + i], got[k, i])
            came[k, i] = lax.ppermute(part, "occ", OVER[1 - k])
    out = []
    for k in range(2):
        for i in range(2):
            out.append(0.5 * (partial_sum(k, i, place, keep_t, integrals[2 * k + i], got[k, i]) + came[k, i]))
    return jnp.stack(out)


def solution(mesh):
    in_specs = (P(None, "occ", "vir"), P(None, "vir", "occ"))
    out_specs = P(None, "occ", "vir")
    body = hybrid_body if dict(mesh.shape) == MESH else gather_body
    return jax.shard_map(body, mesh=mesh, in_specs=in_specs, out_specs=out_specs, check_vma=False)
```

```python
import functools

import jax
import jax.numpy as jnp
from jax import lax
from jax.experimental import pallas as pl
from jax.experimental.pallas import tpu as pltpu
from jax.sharding import PartitionSpec as P

MESH = {"occ": 4, "vir": 8}
STEP = 256


def contract_block(left, piece):
    return lax.dot_general(
        left,
        piece,
        (((2,), (2,)), ((0,), (0,))),
        precision=lax.Precision.HIGHEST,
        preferred_element_type=jnp.float32,
    )


def gather_body(amplitudes, integrals):
    gathered = lax.all_gather(amplitudes, "vir", axis=2, tiled=True)
    panel_sum = contract_block(gathered, lax.all_gather(integrals, "occ", axis=2, tiled=True))
    return 0.5 * panel_sum


BOTH = ("occ", "vir")
X, Y = 1, 2


def pairs(move):
    return [(o * 8 + v, move(o, v >> 1, v & 1)) for o in range(4) for v in range(8)]


SAME_CORE = pairs(lambda o, z, c: (o ^ (X if c else Y)) * 8 + 2 * z + c)
CROSS_CORE = pairs(lambda o, z, c: (o ^ (Y if c else X)) * 8 + 2 * z + 1 - c)
FIRST_Z = pairs(lambda o, z, c: o * 8 + 2 * (z ^ (1 if c else 2)) + c)
SECOND_Z = pairs(lambda o, z, c: o * 8 + 2 * (z ^ (2 if c else 1)) + c)
OVER_CORE = pairs(lambda o, z, c: o * 8 + 2 * z + 1 - c)
FIRST_KIND = pairs(lambda o, z, c: (o ^ (Y if c else X)) * 8 + 2 * z + c)
SECOND_KIND = SAME_CORE

VMEM, HBM = pl.BlockSpec(memory_space=pltpu.VMEM), pl.BlockSpec(memory_space=pl.ANY)


def call(kernel, out_shape, in_specs, out_specs, flops, *args, **more):
    arrays = [*args, *jax.tree.leaves(out_shape)]
    return pl.pallas_call(
        kernel,
        out_shape=out_shape,
        in_specs=in_specs,
        out_specs=out_specs,
        compiler_params=pltpu.CompilerParams(vmem_limit_bytes=16 * 1024 * 1024),
        cost_estimate=pl.CostEstimate(flops=flops, bytes_accessed=4 * sum(a.size for a in arrays), transcendentals=0),
        **more,
    )(*args)


def like(a, *shape):
    return jax.ShapeDtypeStruct(shape, a.dtype)


def position():
    o, v = lax.axis_index("occ"), lax.axis_index("vir")
    return o // 2, lax.rem(o, 2), v // 2, lax.rem(v, 2)


def holds():
    y, x, z, core = position()
    return jnp.where(core == 0, z // 2 == y, lax.rem(z, 2) == x)


def kinds_kernel(whole, first, second, sems):
    core = position()[3]
    copies = [
        pltpu.make_async_copy(whole.at[pl.ds(2 * core, 2)], first, sems.at[0]),
        pltpu.make_async_copy(whole.at[pl.ds(2 - 2 * core, 2)], second, sems.at[1]),
    ]
    for copy in copies:
        copy.start()
    for copy in copies:
        copy.wait()


def kinds(a):
    half = like(a, 2, *a.shape[1:])
    return call(kinds_kernel, (half, half), [HBM], (VMEM, VMEM), 0, a, scratch_shapes=[pltpu.SemaphoreType.DMA((2,))])


def merge_kernel(first, second, out):
    core = position()[3]
    out[core] = first[...]
    out[1 - core] = second[...]


def merge(first, second):
    return call(merge_kernel, like(first, 2, *first.shape), [VMEM] * 2, VMEM, 0, first, second)


def choose_kernel(held, got, out):
    out[...] = jnp.where(holds(), held[...], got[...])


def choose(held, got):
    return call(choose_kernel, like(held, *held.shape), [VMEM] * 2, VMEM, 0, held, got)


def split(a):
    high = a.astype(jnp.bfloat16)
    low = (a - high.astype(jnp.float32)).astype(jnp.bfloat16)
    return high, low


def dot3(left, right):
    (lh, ll), (rh, rl) = left, right

    def dot(a, b):
        return lax.dot_general(a, b, (((1,), (1,)), ((), ())), preferred_element_type=jnp.float32)

    return dot(lh, rh) + (dot(lh, rl) + dot(ll, rh))


def partial_kernel(order, near, far, own, got, out):
    y, x, z, core = position()
    kind = core if order == 0 else 1 - core
    in_order = jnp.where(kind == 0, lax.rem(z, 2) == x, z // 2 == y)
    n_ab = own.shape[1]
    for i in range(2):
        first, second = (jnp.concatenate([a[0, i], a[1, i]], axis=1) for a in (near, far))
        t = split(jnp.concatenate([jnp.where(in_order, first, second), jnp.where(in_order, second, first)], axis=1))
        for low in range(0, n_ab, STEP):
            high = min(low + STEP, n_ab)
            v = split(jnp.concatenate([own[i, low:high, :], got[i, low:high, :]], axis=1))
            out[i, :, low:high] = dot3(t, v)


def partial_sum(order, near, far, own, got):
    n_ij, (n_g, n_ab, n_o) = near.shape[2], own.shape
    flops = 12 * n_g * n_ij * n_ab * n_o
    return call(functools.partial(partial_kernel, order), like(own, n_g, n_ij, n_ab), [VMEM] * 4, VMEM, flops, near, far, own, got)


def finish_kernel(order, kept, came, *refs):
    out, result, sems = refs[-3:]
    core = position()[3]
    kind = core if order == 0 else 1 - core
    copies = []
    for i in range(2):
        result[i] = 0.5 * (kept[i] + came[i])
        copies.append(pltpu.make_async_copy(result.at[i], out.at[2 * kind + i], sems.at[i]))
        copies[-1].start()
    for copy in copies:
        copy.wait()


def finish(order, kept, came, *out):
    n_g, *rest = kept.shape
    return call(
        functools.partial(finish_kernel, order),
        like(kept, 2 * n_g, *rest),
        [VMEM, VMEM] + [HBM] * len(out),
        HBM,
        2 * kept.size,
        kept,
        came,
        *out,
        scratch_shapes=[pltpu.VMEM(kept.shape, jnp.float32), pltpu.SemaphoreType.DMA((2,))],
        input_output_aliases={2: 0} if out else {},
    )


def tie(a, *others):
    return lax.optimization_barrier((a, *others))[0]


def permute(a, perm):
    return lax.ppermute(a, BOTH, perm)


def spread(held):
    near = choose(held, permute(held, FIRST_Z))
    near_other = permute(near, OVER_CORE)
    far = permute(tie(near, near_other), SECOND_Z)
    return [[near, far], [near_other, permute(far, OVER_CORE)]]


def hybrid_body(amplitudes, integrals):
    mine, give = kinds(amplitudes)
    same, cross = permute(mine, SAME_CORE), permute(give, CROSS_CORE)
    halves = kinds(integrals)
    send = spread(merge(tie(same, *halves), cross))
    own = [tie(halves[0], same, cross), tie(halves[1], send[0][0])]
    got = [permute(a, perm) for a, perm in zip(own, (FIRST_KIND, SECOND_KIND))]
    came = []
    for order, perm in enumerate((SECOND_KIND, FIRST_KIND)):
        came.append(permute(partial_sum(order, *send[order], own[order], got[order]), perm))

    keep = spread(tie(merge(mine, permute(tie(give, send[0][0]), OVER_CORE)), send[0][1]))
    out = []
    for order in range(2):
        kept = partial_sum(order, *keep[order], own[order], got[order])
        out = [finish(order, kept, came[order], *out)]
    return out[0]


def solution(mesh):
    in_specs = (P(None, "occ", "vir"), P(None, "vir", "occ"))
    out_specs = P(None, "occ", "vir")
    body = hybrid_body if dict(mesh.shape) == MESH else gather_body
    return jax.shard_map(body, mesh=mesh, in_specs=in_specs, out_specs=out_specs, check_vma=False)
```

```python
import functools

import jax
import jax.numpy as jnp
from jax import lax
from jax.experimental import pallas as pl
from jax.experimental.pallas import tpu as pltpu
from jax.sharding import PartitionSpec as P

MESH = {"occ": 4, "vir": 8}
STEP = 256
CUTS = (), (512,)


def contract_block(left, piece):
    return lax.dot_general(
        left,
        piece,
        (((2,), (2,)), ((0,), (0,))),
        precision=lax.Precision.HIGHEST,
        preferred_element_type=jnp.float32,
    )


def gather_body(amplitudes, integrals):
    gathered = lax.all_gather(amplitudes, "vir", axis=2, tiled=True)
    panel_sum = contract_block(gathered, lax.all_gather(integrals, "occ", axis=2, tiled=True))
    return 0.5 * panel_sum


BOTH = ("occ", "vir")
X, Y = 1, 2


def pairs(move):
    return [(o * 8 + v, move(o, v >> 1, v & 1)) for o in range(4) for v in range(8)]


SAME_CORE = pairs(lambda o, z, c: (o ^ (X if c else Y)) * 8 + 2 * z + c)
CROSS_CORE = pairs(lambda o, z, c: (o ^ (Y if c else X)) * 8 + 2 * z + 1 - c)
FIRST_Z = pairs(lambda o, z, c: o * 8 + 2 * (z ^ (1 if c else 2)) + c)
SECOND_Z = pairs(lambda o, z, c: o * 8 + 2 * (z ^ (2 if c else 1)) + c)
OVER_CORE = pairs(lambda o, z, c: o * 8 + 2 * z + 1 - c)
FIRST_KIND = pairs(lambda o, z, c: (o ^ (Y if c else X)) * 8 + 2 * z + c)
SECOND_KIND = SAME_CORE

VMEM, HBM = pl.BlockSpec(memory_space=pltpu.VMEM), pl.BlockSpec(memory_space=pl.ANY)


def call(kernel, out_shape, in_specs, out_specs, flops, *args, **more):
    arrays = [*args, *jax.tree.leaves(out_shape)]
    return pl.pallas_call(
        kernel,
        out_shape=out_shape,
        in_specs=in_specs,
        out_specs=out_specs,
        compiler_params=pltpu.CompilerParams(vmem_limit_bytes=16 * 1024 * 1024),
        cost_estimate=pl.CostEstimate(flops=flops, bytes_accessed=4 * sum(a.size for a in arrays), transcendentals=0),
        **more,
    )(*args)


def like(a, *shape):
    return jax.ShapeDtypeStruct(shape, a.dtype)


def position():
    o, v = lax.axis_index("occ"), lax.axis_index("vir")
    return o // 2, lax.rem(o, 2), v // 2, lax.rem(v, 2)


def holds():
    y, x, z, core = position()
    return jnp.where(core == 0, z // 2 == y, lax.rem(z, 2) == x)


def kinds_kernel(spans, whole, *refs):
    *out, sems = refs
    core = position()[3]
    copies = []
    for ref, (order, low, high) in zip(out, spans):
        kind = core if order == 0 else 1 - core
        source = whole.at[pl.ds(2 * kind, 2), pl.ds(low, high - low)]
        copies.append(pltpu.make_async_copy(source, ref, sems.at[len(copies)]))
    for copy in copies:
        copy.start()
    for copy in copies:
        copy.wait()


def kinds(a, *cuts):
    n = a.shape[1]
    spans = [(order, low, high) for order, cut in enumerate(cuts) for low, high in zip((0, *cut), (*cut, n))]
    out = [like(a, 2, high - low, a.shape[2]) for _, low, high in spans]
    sems = pltpu.SemaphoreType.DMA((len(spans),))
    pieces = call(functools.partial(kinds_kernel, spans), out, [HBM], [VMEM] * len(out), 0, a, scratch_shapes=[sems])
    return [[p for p, span in zip(pieces, spans) if span[0] == order] for order in range(2)]


def merge_kernel(first, second, out):
    core = position()[3]
    out[core] = first[...]
    out[1 - core] = second[...]


def merge(first, second):
    return call(merge_kernel, like(first, 2, *first.shape), [VMEM] * 2, VMEM, 0, first, second)


def choose_kernel(held, got, out, *small):
    out[...] = jnp.where(holds(), held[...], got[...])
    for ref in small:
        ref[...] = out[0, 0, : ref.shape[0], :]


def choose(held, got, *small):
    shapes = [like(held, *held.shape)] + [like(held, 8, held.shape[3])] * len(small)
    return call(choose_kernel, shapes, [VMEM] * 2, [VMEM] * len(shapes), 0, held, got)


def gate_kernel(a, small, out):
    del a, small, out


def gate(a, small):
    return call(gate_kernel, like(a, *a.shape), [HBM] * 2, HBM, 0, a, small, input_output_aliases={0: 0})


def split(a):
    high = a.astype(jnp.bfloat16)
    low = (a - high.astype(jnp.float32)).astype(jnp.bfloat16)
    return high, low


def dot3(left, right):
    (lh, ll), (rh, rl) = left, right

    def dot(a, b):
        return lax.dot_general(a, b, (((1,), (1,)), ((), ())), preferred_element_type=jnp.float32)

    return dot(lh, rh) + (dot(lh, rl) + dot(ll, rh))


def partial_kernel(order, near, far, *refs):
    *chunks, out = refs
    y, x, z, core = position()
    kind = core if order == 0 else 1 - core
    in_order = jnp.where(kind == 0, lax.rem(z, 2) == x, z // 2 == y)
    for i in range(2):
        first, second = (jnp.concatenate([a[0, i], a[1, i]], axis=1) for a in (near, far))
        t = split(jnp.concatenate([jnp.where(in_order, first, second), jnp.where(in_order, second, first)], axis=1))
        at = 0
        for own, got in zip(chunks[::2], chunks[1::2]):
            n_ab = own.shape[1]
            for low in range(0, n_ab, STEP):
                high = min(low + STEP, n_ab)
                v = split(jnp.concatenate([own[i, low:high, :], got[i, low:high, :]], axis=1))
                out[i, :, at : at + high - low] = dot3(t, v)
                at += high - low


def partial_sum(order, near, far, own, got):
    n_ij, (n_g, _, n_o), n_ab = near.shape[2], own[0].shape, sum(a.shape[1] for a in own)
    chunks = [a for pair in zip(own, got) for a in pair]
    flops = 12 * n_g * n_ij * n_ab * n_o
    specs = [VMEM] * (2 + len(chunks))
    return call(functools.partial(partial_kernel, order), like(near, n_g, n_ij, n_ab), specs, VMEM, flops, near, far, *chunks)


def finish_kernel(order, kept, came, *refs):
    out, result, sems = refs[-3:]
    core = position()[3]
    kind = core if order == 0 else 1 - core
    copies = []
    for i in range(2):
        result[i] = 0.5 * (kept[i] + came[i])
        copies.append(pltpu.make_async_copy(result.at[i], out.at[2 * kind + i], sems.at[i]))
        copies[-1].start()
    for copy in copies:
        copy.wait()


def finish(order, kept, came, *out):
    n_g, *rest = kept.shape
    return call(
        functools.partial(finish_kernel, order),
        like(kept, 2 * n_g, *rest),
        [VMEM, VMEM] + [HBM] * len(out),
        HBM,
        2 * kept.size,
        kept,
        came,
        *out,
        scratch_shapes=[pltpu.VMEM(kept.shape, jnp.float32), pltpu.SemaphoreType.DMA((2,))],
        input_output_aliases={2: 0} if out else {},
    )


def tie(a, *others):
    return lax.optimization_barrier((a, *others))[0]


def permute(a, perm):
    return lax.ppermute(a, BOTH, perm)


def spread(held, short):
    if short:
        near, small = choose(held, permute(held, FIRST_Z), 1)
        near = gate(near, permute(small, OVER_CORE))
        near_other = permute(near, OVER_CORE)
        far = permute(near, SECOND_Z)
    else:
        (near,) = choose(held, permute(held, FIRST_Z))
        near_other = permute(near, OVER_CORE)
        far = permute(tie(near, near_other), SECOND_Z)
    return [[near, far], [near_other, permute(far, OVER_CORE)]]


def hybrid_body(amplitudes, integrals):
    (mine,), (give,) = kinds(amplitudes, (), ())
    same, cross = permute(mine, SAME_CORE), permute(give, CROSS_CORE)
    own = kinds(integrals, *CUTS)
    send = spread(merge(tie(same, *own[0], *own[1]), cross), True)
    own[0] = [tie(a, same, cross) for a in own[0]]
    own[1] = [tie(a, send[0][0]) for a in own[1]]
    got = [[permute(a, perm) for a in pieces] for pieces, perm in zip(own, (FIRST_KIND, SECOND_KIND))]
    came = []
    for order, perm in enumerate((SECOND_KIND, FIRST_KIND)):
        came.append(permute(partial_sum(order, *send[order], own[order], got[order]), perm))

    keep = spread(tie(merge(mine, permute(tie(give, send[0][0]), OVER_CORE)), send[0][1]), False)
    out = []
    for order in range(2):
        kept = partial_sum(order, *keep[order], own[order], got[order])
        out = [finish(order, kept, came[order], *out)]
    return out[0]


def solution(mesh):
    in_specs = (P(None, "occ", "vir"), P(None, "vir", "occ"))
    out_specs = P(None, "occ", "vir")
    body = hybrid_body if dict(mesh.shape) == MESH else gather_body
    return jax.shard_map(body, mesh=mesh, in_specs=in_specs, out_specs=out_specs, check_vma=False)
```

```python
import functools

import jax
import jax.numpy as jnp
from jax import lax
from jax.experimental import pallas as pl
from jax.experimental.pallas import tpu as pltpu
from jax.sharding import PartitionSpec as P

MESH = {"occ": 4, "vir": 8}
STEP = 256


def contract_block(left, piece):
    return lax.dot_general(
        left,
        piece,
        (((2,), (2,)), ((0,), (0,))),
        precision=lax.Precision.HIGHEST,
        preferred_element_type=jnp.float32,
    )


def gather_body(amplitudes, integrals):
    gathered = lax.all_gather(amplitudes, "vir", axis=2, tiled=True)
    panel_sum = contract_block(gathered, lax.all_gather(integrals, "occ", axis=2, tiled=True))
    return 0.5 * panel_sum


BOTH = ("occ", "vir")
X, Y = 1, 2


def pairs(move):
    return [(o * 8 + v, move(o, v >> 1, v & 1)) for o in range(4) for v in range(8)]


SAME_CORE = pairs(lambda o, z, c: (o ^ (X if c else Y)) * 8 + 2 * z + c)
CROSS_CORE = pairs(lambda o, z, c: (o ^ (Y if c else X)) * 8 + 2 * z + 1 - c)
FIRST_Z = pairs(lambda o, z, c: o * 8 + 2 * (z ^ (1 if c else 2)) + c)
SECOND_Z = pairs(lambda o, z, c: o * 8 + 2 * (z ^ (2 if c else 1)) + c)
OVER_CORE = pairs(lambda o, z, c: o * 8 + 2 * z + 1 - c)
FIRST_KIND = pairs(lambda o, z, c: (o ^ (Y if c else X)) * 8 + 2 * z + c)
SECOND_KIND = SAME_CORE

VMEM, HBM = pl.BlockSpec(memory_space=pltpu.VMEM), pl.BlockSpec(memory_space=pl.ANY)


def call(kernel, out_shape, in_specs, out_specs, flops, *args, **more):
    arrays = [*args, *jax.tree.leaves(out_shape)]
    return pl.pallas_call(
        kernel,
        out_shape=out_shape,
        in_specs=in_specs,
        out_specs=out_specs,
        compiler_params=pltpu.CompilerParams(vmem_limit_bytes=16 * 1024 * 1024),
        cost_estimate=pl.CostEstimate(flops=flops, bytes_accessed=4 * sum(a.size for a in arrays), transcendentals=0),
        **more,
    )(*args)


def like(a, *shape):
    return jax.ShapeDtypeStruct(shape, a.dtype)


def position():
    o, v = lax.axis_index("occ"), lax.axis_index("vir")
    return o // 2, lax.rem(o, 2), v // 2, lax.rem(v, 2)


def holds():
    y, x, z, core = position()
    return jnp.where(core == 0, z // 2 == y, lax.rem(z, 2) == x)


def kinds_kernel(spans, whole, *refs):
    *out, sems = refs
    core = position()[3]
    copies = []
    for ref, (order, low, high) in zip(out, spans):
        kind = core if order == 0 else 1 - core
        source = whole.at[pl.ds(2 * kind, 2), pl.ds(low, high - low)]
        copies.append(pltpu.make_async_copy(source, ref, sems.at[len(copies)]))
    for copy in copies:
        copy.start()
    for copy in copies:
        copy.wait()


def kinds(a, *cuts):
    n = a.shape[1]
    spans = [(order, low, high) for order, cut in enumerate(cuts) for low, high in zip((0, *cut), (*cut, n))]
    out = [like(a, 2, high - low, a.shape[2]) for _, low, high in spans]
    sems = pltpu.SemaphoreType.DMA((len(spans),))
    pieces = call(functools.partial(kinds_kernel, spans), out, [HBM], [VMEM] * len(out), 0, a, scratch_shapes=[sems])
    return [[p for p, span in zip(pieces, spans) if span[0] == order] for order in range(2)]


def merge_kernel(first, second, out):
    core = position()[3]
    out[core] = first[...]
    out[1 - core] = second[...]


def merge(first, second):
    return call(merge_kernel, like(first, 2, *first.shape), [VMEM] * 2, VMEM, 0, first, second)


def choose_kernel(held, got, out, *small):
    out[...] = jnp.where(holds(), held[...], got[...])
    for ref in small:
        ref[...] = out[0, 0, : ref.shape[0], :]


def choose(held, got, *small):
    shapes = [like(held, *held.shape)] + [like(held, 8, held.shape[3])] * len(small)
    return call(choose_kernel, shapes, [VMEM] * 2, [VMEM] * len(shapes), 0, held, got)


def gate_kernel(a, small, out):
    del a, small, out


def gate(a, small):
    return call(gate_kernel, like(a, *a.shape), [HBM] * 2, HBM, 0, a, small, input_output_aliases={0: 0})


def split(a):
    high = a.astype(jnp.bfloat16)
    low = (a - high.astype(jnp.float32)).astype(jnp.bfloat16)
    return high, low


def dot3(left, right):
    (lh, ll), (rh, rl) = left, right

    def dot(a, b):
        return lax.dot_general(a, b, (((1,), (1,)), ((), ())), preferred_element_type=jnp.float32)

    return dot(lh, rh) + (dot(lh, rl) + dot(ll, rh))


def partial_kernel(order, near, far, *refs):
    *chunks, out = refs
    y, x, z, core = position()
    kind = core if order == 0 else 1 - core
    in_order = jnp.where(kind == 0, lax.rem(z, 2) == x, z // 2 == y)
    for i in range(2):
        first, second = (jnp.concatenate([a[0, i], a[1, i]], axis=1) for a in (near, far))
        t = split(jnp.concatenate([jnp.where(in_order, first, second), jnp.where(in_order, second, first)], axis=1))
        at = 0
        for own, got in zip(chunks[::2], chunks[1::2]):
            n_ab = own.shape[1]
            for low in range(0, n_ab, STEP):
                high = min(low + STEP, n_ab)
                v = split(jnp.concatenate([own[i, low:high, :], got[i, low:high, :]], axis=1))
                out[i, :, at : at + high - low] = dot3(t, v)
                at += high - low


def partial_sum(order, near, far, own, got):
    n_ij, (n_g, _, n_o), n_ab = near.shape[2], own[0].shape, sum(a.shape[1] for a in own)
    chunks = [a for pair in zip(own, got) for a in pair]
    flops = 12 * n_g * n_ij * n_ab * n_o
    specs = [VMEM] * (2 + len(chunks))
    return call(functools.partial(partial_kernel, order), like(near, n_g, n_ij, n_ab), specs, VMEM, flops, near, far, *chunks)


def finish_kernel(order, kept, came, *refs):
    out, result, sems = refs[-3:]
    core = position()[3]
    kind = core if order == 0 else 1 - core
    copies = []
    for i in range(2):
        result[i] = 0.5 * (kept[i] + came[i])
        copies.append(pltpu.make_async_copy(result.at[i], out.at[2 * kind + i], sems.at[i]))
        copies[-1].start()
    for copy in copies:
        copy.wait()


def finish(order, kept, came, *out):
    n_g, *rest = kept.shape
    return call(
        functools.partial(finish_kernel, order),
        like(kept, 2 * n_g, *rest),
        [VMEM, VMEM] + [HBM] * len(out),
        HBM,
        2 * kept.size,
        kept,
        came,
        *out,
        scratch_shapes=[pltpu.VMEM(kept.shape, jnp.float32), pltpu.SemaphoreType.DMA((2,))],
        input_output_aliases={2: 0} if out else {},
    )


def tie(a, *others):
    return lax.optimization_barrier((a, *others))[0]


def permute(a, perm):
    return lax.ppermute(a, BOTH, perm)


def spread(held, short):
    if short:
        near, small = choose(held, permute(held, FIRST_Z), 1)
        near = gate(near, permute(small, OVER_CORE))
        near_other = permute(near, OVER_CORE)
        far = permute(near, SECOND_Z)
    else:
        (near,) = choose(held, permute(held, FIRST_Z))
        near_other = permute(near, OVER_CORE)
        far = permute(tie(near, near_other), SECOND_Z)
    return [[near, far], [near_other, permute(far, OVER_CORE)]]


def hybrid_body(amplitudes, integrals):
    (mine,), (give,) = kinds(amplitudes, (), ())
    same, cross = permute(mine, SAME_CORE), permute(give, CROSS_CORE)
    n_ab = integrals.shape[1]
    own = kinds(integrals, (n_ab * 25 // 28,), (n_ab * 9 // 14,))
    send = spread(merge(tie(same, *own[0], *own[1]), cross), True)

    own[1] = [tie(a, send[0][0]) for a in own[1]]
    got = [[permute(a, perm) for a in pieces] for pieces, perm in zip(own, (FIRST_KIND, SECOND_KIND))]
    came = []
    for order, perm in enumerate((SECOND_KIND, FIRST_KIND)):
        came.append(permute(partial_sum(order, *send[order], own[order], got[order]), perm))

    keep = spread(tie(merge(mine, permute(tie(give, send[0][0]), OVER_CORE)), send[0][1]), False)
    out = []
    for order in range(2):
        kept = partial_sum(order, *keep[order], own[order], got[order])
        out = [finish(order, kept, came[order], *out)]
    return out[0]


def solution(mesh):
    in_specs = (P(None, "occ", "vir"), P(None, "vir", "occ"))
    out_specs = P(None, "occ", "vir")
    body = hybrid_body if dict(mesh.shape) == MESH else gather_body
    return jax.shard_map(body, mesh=mesh, in_specs=in_specs, out_specs=out_specs, check_vma=False)
```

```python
import functools

import jax
import jax.numpy as jnp
from jax import lax
from jax.experimental import pallas as pl
from jax.experimental.pallas import tpu as pltpu
from jax.sharding import PartitionSpec as P

MESH = {"occ": 4, "vir": 8}
STEP = 256


def contract_block(left, piece):
    return lax.dot_general(
        left,
        piece,
        (((2,), (2,)), ((0,), (0,))),
        precision=lax.Precision.HIGHEST,
        preferred_element_type=jnp.float32,
    )


def gather_body(amplitudes, integrals):
    gathered = lax.all_gather(amplitudes, "vir", axis=2, tiled=True)
    panel_sum = contract_block(gathered, lax.all_gather(integrals, "occ", axis=2, tiled=True))
    return 0.5 * panel_sum


BOTH = ("occ", "vir")
X, Y = 1, 2


def pairs(move):
    return [(o * 8 + v, move(o, v >> 1, v & 1)) for o in range(4) for v in range(8)]


SAME_CORE = pairs(lambda o, z, c: (o ^ (X if c else Y)) * 8 + 2 * z + c)
CROSS_CORE = pairs(lambda o, z, c: (o ^ (Y if c else X)) * 8 + 2 * z + 1 - c)
FIRST_Z = pairs(lambda o, z, c: o * 8 + 2 * (z ^ (1 if c else 2)) + c)
SECOND_Z = pairs(lambda o, z, c: o * 8 + 2 * (z ^ (2 if c else 1)) + c)
OVER_CORE = pairs(lambda o, z, c: o * 8 + 2 * z + 1 - c)
FIRST_KIND = pairs(lambda o, z, c: (o ^ (Y if c else X)) * 8 + 2 * z + c)
SECOND_KIND = SAME_CORE

VMEM, HBM = pl.BlockSpec(memory_space=pltpu.VMEM), pl.BlockSpec(memory_space=pl.ANY)


def call(kernel, out_shape, in_specs, out_specs, flops, *args, **more):
    arrays = [*args, *jax.tree.leaves(out_shape)]
    return pl.pallas_call(
        kernel,
        out_shape=out_shape,
        in_specs=in_specs,
        out_specs=out_specs,
        compiler_params=pltpu.CompilerParams(vmem_limit_bytes=16 * 1024 * 1024),
        cost_estimate=pl.CostEstimate(flops=flops, bytes_accessed=4 * sum(a.size for a in arrays), transcendentals=0),
        **more,
    )(*args)


def like(a, *shape):
    return jax.ShapeDtypeStruct(shape, a.dtype)


def position():
    o, v = lax.axis_index("occ"), lax.axis_index("vir")
    return o // 2, lax.rem(o, 2), v // 2, lax.rem(v, 2)


def holds():
    y, x, z, core = position()
    return jnp.where(core == 0, z // 2 == y, lax.rem(z, 2) == x)


def kinds_kernel(spans, whole, *refs):
    *out, sems = refs
    core = position()[3]
    copies = []
    for ref, (order, low, high) in zip(out, spans):
        kind = core if order == 0 else 1 - core
        source = whole.at[pl.ds(2 * kind, 2), pl.ds(low, high - low)]
        copies.append(pltpu.make_async_copy(source, ref, sems.at[len(copies)]))
    for copy in copies:
        copy.start()
    for copy in copies:
        copy.wait()


def kinds(a, *cuts):
    n = a.shape[1]
    spans = [(order, low, high) for order, cut in enumerate(cuts) for low, high in zip((0, *cut), (*cut, n))]
    out = [like(a, 2, high - low, a.shape[2]) for _, low, high in spans]
    sems = pltpu.SemaphoreType.DMA((len(spans),))
    pieces = call(functools.partial(kinds_kernel, spans), out, [HBM], [VMEM] * len(out), 0, a, scratch_shapes=[sems])
    return [[p for p, span in zip(pieces, spans) if span[0] == order] for order in range(2)]


def merge_kernel(first, second, out):
    core = position()[3]
    out[core] = first[...]
    out[1 - core] = second[...]


def merge(first, second):
    return call(merge_kernel, like(first, 2, *first.shape), [VMEM] * 2, VMEM, 0, first, second)


def choose_kernel(held, got, out, *small):
    out[...] = jnp.where(holds(), held[...], got[...])
    for ref in small:
        ref[...] = out[0, 0, : ref.shape[0], :]


def choose(held, got, *small):
    shapes = [like(held, *held.shape)] + [like(held, 8, held.shape[3])] * len(small)
    return call(choose_kernel, shapes, [VMEM] * 2, [VMEM] * len(shapes), 0, held, got)


def gate_kernel(a, small, out):
    del a, small, out


def gate(a, small):
    return call(gate_kernel, like(a, *a.shape), [HBM] * 2, HBM, 0, a, small, input_output_aliases={0: 0})


def split(a):
    high = a.astype(jnp.bfloat16)
    low = (a - high.astype(jnp.float32)).astype(jnp.bfloat16)
    return high, low


def dot3(left, right):
    (lh, ll), (rh, rl) = left, right

    def dot(a, b):
        return lax.dot_general(a, b, (((1,), (1,)), ((), ())), preferred_element_type=jnp.float32)

    return dot(lh, rh) + (dot(lh, rl) + dot(ll, rh))


def partial_kernel(order, near, far, *refs):
    *chunks, out = refs
    y, x, z, core = position()
    kind = core if order == 0 else 1 - core
    in_order = jnp.where(kind == 0, lax.rem(z, 2) == x, z // 2 == y)
    for i in range(2):
        first, second = (jnp.concatenate([a[0, i], a[1, i]], axis=1) for a in (near, far))
        t = split(jnp.concatenate([jnp.where(in_order, first, second), jnp.where(in_order, second, first)], axis=1))
        at = 0
        for own, got in zip(chunks[::2], chunks[1::2]):
            n_ab = own.shape[1]
            for low in range(0, n_ab, STEP):
                high = min(low + STEP, n_ab)
                v = split(jnp.concatenate([own[i, low:high, :], got[i, low:high, :]], axis=1))
                out[i, :, at : at + high - low] = dot3(t, v)
                at += high - low


def partial_sum(order, near, far, own, got):
    n_ij, (n_g, _, n_o), n_ab = near.shape[2], own[0].shape, sum(a.shape[1] for a in own)
    chunks = [a for pair in zip(own, got) for a in pair]
    flops = 12 * n_g * n_ij * n_ab * n_o
    specs = [VMEM] * (2 + len(chunks))
    return call(functools.partial(partial_kernel, order), like(near, n_g, n_ij, n_ab), specs, VMEM, flops, near, far, *chunks)


def finish_kernel(order, kept, came, *refs):
    out, result, sems = refs[-3:]
    core = position()[3]
    kind = core if order == 0 else 1 - core
    copies = []
    for i in range(2):
        result[i] = 0.5 * (kept[i] + came[i])
        copies.append(pltpu.make_async_copy(result.at[i], out.at[2 * kind + i], sems.at[i]))
        copies[-1].start()
    for copy in copies:
        copy.wait()


def finish(order, kept, came, *out):
    n_g, *rest = kept.shape
    return call(
        functools.partial(finish_kernel, order),
        like(kept, 2 * n_g, *rest),
        [VMEM, VMEM] + [HBM] * len(out),
        HBM,
        2 * kept.size,
        kept,
        came,
        *out,
        scratch_shapes=[pltpu.VMEM(kept.shape, jnp.float32), pltpu.SemaphoreType.DMA((2,))],
        input_output_aliases={2: 0} if out else {},
    )


def tie(a, *others):
    return lax.optimization_barrier((a, *others))[0]


def permute(a, perm):
    return lax.ppermute(a, BOTH, perm)


def spread(held, short):
    if short:
        ready, small = choose(held, permute(held, FIRST_Z), 1)
        near = gate(ready, permute(small, OVER_CORE))
        near_other = permute(near, OVER_CORE)
        far = permute(near, SECOND_Z)
    else:
        (near,) = choose(held, permute(held, FIRST_Z))
        ready = near
        near_other = permute(near, OVER_CORE)
        far = permute(tie(near, near_other), SECOND_Z)
    return [[near, far], [near_other, permute(far, OVER_CORE)]], ready


def hybrid_body(amplitudes, integrals):
    (mine,), (give,) = kinds(amplitudes, (), ())
    same, cross = permute(mine, SAME_CORE), permute(give, CROSS_CORE)
    n_ab = integrals.shape[1]
    own = kinds(integrals, (n_ab * 25 // 28,), (n_ab * 9 // 14,))
    send, ready = spread(merge(tie(same, *own[0], *own[1]), cross), True)

    own[1] = [tie(a, ready) for a in own[1]]
    got = [[permute(a, perm) for a in pieces] for pieces, perm in zip(own, (FIRST_KIND, SECOND_KIND))]
    came = []
    for order, perm in enumerate((SECOND_KIND, FIRST_KIND)):
        came.append(permute(partial_sum(order, *send[order], own[order], got[order]), perm))

    keep, _ = spread(tie(merge(mine, permute(tie(give, send[0][0]), OVER_CORE)), send[0][1]), False)
    out = []
    for order in range(2):
        kept = partial_sum(order, *keep[order], own[order], got[order])
        out = [finish(order, kept, came[order], *out)]
    return out[0]


def solution(mesh):
    in_specs = (P(None, "occ", "vir"), P(None, "vir", "occ"))
    out_specs = P(None, "occ", "vir")
    body = hybrid_body if dict(mesh.shape) == MESH else gather_body
    return jax.shard_map(body, mesh=mesh, in_specs=in_specs, out_specs=out_specs, check_vma=False)
```

```python
import functools

import jax
import jax.numpy as jnp
from jax import lax
from jax.experimental import pallas as pl
from jax.experimental.pallas import tpu as pltpu
from jax.sharding import PartitionSpec as P

MESH = {"occ": 4, "vir": 8}
STEP = 256


def contract_block(left, piece):
    return lax.dot_general(
        left,
        piece,
        (((2,), (2,)), ((0,), (0,))),
        precision=lax.Precision.HIGHEST,
        preferred_element_type=jnp.float32,
    )


def gather_body(amplitudes, integrals):
    gathered = lax.all_gather(amplitudes, "vir", axis=2, tiled=True)
    panel_sum = contract_block(gathered, lax.all_gather(integrals, "occ", axis=2, tiled=True))
    return 0.5 * panel_sum


BOTH = ("occ", "vir")
X, Y = 1, 2


def pairs(move):
    return [(o * 8 + v, move(o, v >> 1, v & 1)) for o in range(4) for v in range(8)]


SAME_CORE = pairs(lambda o, z, c: (o ^ (X if c else Y)) * 8 + 2 * z + c)
CROSS_CORE = pairs(lambda o, z, c: (o ^ (Y if c else X)) * 8 + 2 * z + 1 - c)
FIRST_Z = pairs(lambda o, z, c: o * 8 + 2 * (z ^ (1 if c else 2)) + c)
SECOND_Z = pairs(lambda o, z, c: o * 8 + 2 * (z ^ (2 if c else 1)) + c)
OVER_CORE = pairs(lambda o, z, c: o * 8 + 2 * z + 1 - c)
FIRST_KIND = pairs(lambda o, z, c: (o ^ (Y if c else X)) * 8 + 2 * z + c)
SECOND_KIND = SAME_CORE

VMEM, HBM = pl.BlockSpec(memory_space=pltpu.VMEM), pl.BlockSpec(memory_space=pl.ANY)


def call(kernel, out_shape, in_specs, out_specs, flops, *args, **more):
    arrays = [*args, *jax.tree.leaves(out_shape)]
    return pl.pallas_call(
        kernel,
        out_shape=out_shape,
        in_specs=in_specs,
        out_specs=out_specs,
        compiler_params=pltpu.CompilerParams(vmem_limit_bytes=16 * 1024 * 1024),
        cost_estimate=pl.CostEstimate(flops=flops, bytes_accessed=4 * sum(a.size for a in arrays), transcendentals=0),
        **more,
    )(*args)


def like(a, *shape):
    return jax.ShapeDtypeStruct(shape, a.dtype)


def position():
    o, v = lax.axis_index("occ"), lax.axis_index("vir")
    return o // 2, lax.rem(o, 2), v // 2, lax.rem(v, 2)


def holds():
    y, x, z, core = position()
    return jnp.where(core == 0, z // 2 == y, lax.rem(z, 2) == x)


def kinds_kernel(spans, whole, *refs):
    *out, sems = refs
    core = position()[3]
    copies = []
    for ref, (order, low, high) in zip(out, spans):
        kind = core if order == 0 else 1 - core
        source = whole.at[pl.ds(2 * kind, 2), pl.ds(low, high - low)]
        copies.append(pltpu.make_async_copy(source, ref, sems.at[len(copies)]))
    for copy in copies:
        copy.start()
    for copy in copies:
        copy.wait()


def kinds(a, *cuts):
    n = a.shape[1]
    spans = [(order, low, high) for order, cut in enumerate(cuts) for low, high in zip((0, *cut), (*cut, n))]
    out = [like(a, 2, high - low, a.shape[2]) for _, low, high in spans]
    sems = pltpu.SemaphoreType.DMA((len(spans),))
    pieces = call(functools.partial(kinds_kernel, spans), out, [HBM], [VMEM] * len(out), 0, a, scratch_shapes=[sems])
    return [[p for p, span in zip(pieces, spans) if span[0] == order] for order in range(2)]


def merge_kernel(first, second, out):
    core = position()[3]
    out[core] = first[...]
    out[1 - core] = second[...]


def merge(first, second):
    return call(merge_kernel, like(first, 2, *first.shape), [VMEM] * 2, VMEM, 0, first, second)


def choose_kernel(held, got, out, *small):
    out[...] = jnp.where(holds(), held[...], got[...])
    for ref in small:
        ref[...] = out[0, 0, : ref.shape[0], :]


def choose(held, got, *small):
    shapes = [like(held, *held.shape)] + [like(held, 8, held.shape[3])] * len(small)
    return call(choose_kernel, shapes, [VMEM] * 2, [VMEM] * len(shapes), 0, held, got)


def gate_kernel(a, small, out):
    del a, small, out


def gate(a, small):
    return call(gate_kernel, like(a, *a.shape), [HBM] * 2, HBM, 0, a, small, input_output_aliases={0: 0})


def split(a):
    high = a.astype(jnp.bfloat16)
    low = (a - high.astype(jnp.float32)).astype(jnp.bfloat16)
    return high, low


def dot3(left, right):
    (lh, ll), (rh, rl) = left, right

    def dot(a, b):
        return lax.dot_general(a, b, (((1,), (1,)), ((), ())), preferred_element_type=jnp.float32)

    return dot(lh, rh) + (dot(lh, rl) + dot(ll, rh))


def partial_kernel(order, near, far, *refs):
    *chunks, out = refs
    y, x, z, core = position()
    kind = core if order == 0 else 1 - core
    in_order = jnp.where(kind == 0, lax.rem(z, 2) == x, z // 2 == y)
    for i in range(2):
        first, second = (jnp.concatenate([a[0, i], a[1, i]], axis=1) for a in (near, far))
        t = split(jnp.concatenate([jnp.where(in_order, first, second), jnp.where(in_order, second, first)], axis=1))
        at = 0
        for own, got in zip(chunks[::2], chunks[1::2]):
            n_ab = own.shape[1]
            for low in range(0, n_ab, STEP):
                high = min(low + STEP, n_ab)
                v = split(jnp.concatenate([own[i, low:high, :], got[i, low:high, :]], axis=1))
                out[i, :, at : at + high - low] = dot3(t, v)
                at += high - low


def partial_sum(order, near, far, own, got):
    n_ij, (n_g, _, n_o), n_ab = near.shape[2], own[0].shape, sum(a.shape[1] for a in own)
    chunks = [a for pair in zip(own, got) for a in pair]
    flops = 12 * n_g * n_ij * n_ab * n_o
    specs = [VMEM] * (2 + len(chunks))
    return call(functools.partial(partial_kernel, order), like(near, n_g, n_ij, n_ab), specs, VMEM, flops, near, far, *chunks)


def finish_kernel(order, kept, came, *refs):
    out, result, sems = refs[-3:]
    core = position()[3]
    kind = core if order == 0 else 1 - core
    copies = []
    for i in range(2):
        result[i] = 0.5 * (kept[i] + came[i])
        copies.append(pltpu.make_async_copy(result.at[i], out.at[2 * kind + i], sems.at[i]))
        copies[-1].start()
    for copy in copies:
        copy.wait()


def finish(order, kept, came, *out):
    n_g, *rest = kept.shape
    return call(
        functools.partial(finish_kernel, order),
        like(kept, 2 * n_g, *rest),
        [VMEM, VMEM] + [HBM] * len(out),
        HBM,
        2 * kept.size,
        kept,
        came,
        *out,
        scratch_shapes=[pltpu.VMEM(kept.shape, jnp.float32), pltpu.SemaphoreType.DMA((2,))],
        input_output_aliases={2: 0} if out else {},
    )


def tie(a, *others):
    return lax.optimization_barrier((a, *others))[0]


def permute(a, perm):
    return lax.ppermute(a, BOTH, perm)


def spread(held, short):
    if short:
        ready, small = choose(held, permute(held, FIRST_Z), 1)
        near = gate(ready, permute(small, OVER_CORE))
        near_other = permute(near, OVER_CORE)
        far = permute(near, SECOND_Z)
    else:
        (near,) = choose(held, permute(held, FIRST_Z))
        ready = near
        near_other = permute(near, OVER_CORE)
        far = permute(tie(near, near_other), SECOND_Z)
    return [[near, far], [near_other, permute(far, OVER_CORE)]], ready


def hybrid_body(amplitudes, integrals):
    (mine,), (give,) = kinds(amplitudes, (), ())
    same, cross = permute(mine, SAME_CORE), permute(give, CROSS_CORE)
    n_ab = integrals.shape[1]
    own = kinds(integrals, (n_ab * 51 // 56,), (n_ab * 19 // 28,))
    send, ready = spread(merge(tie(same, *own[0], *own[1]), cross), True)

    own[1] = [tie(a, ready) for a in own[1]]
    got = [[permute(a, perm) for a in pieces] for pieces, perm in zip(own, (FIRST_KIND, SECOND_KIND))]
    came = []
    for order, perm in enumerate((SECOND_KIND, FIRST_KIND)):
        came.append(permute(partial_sum(order, *send[order], own[order], got[order]), perm))

    keep, _ = spread(tie(merge(mine, permute(tie(give, send[0][0]), OVER_CORE)), send[0][1]), False)
    out = []
    for order in range(2):
        kept = partial_sum(order, *keep[order], own[order], got[order])
        out = [finish(order, kept, came[order], *out)]
    return out[0]


def solution(mesh):
    in_specs = (P(None, "occ", "vir"), P(None, "vir", "occ"))
    out_specs = P(None, "occ", "vir")
    body = hybrid_body if dict(mesh.shape) == MESH else gather_body
    return jax.shard_map(body, mesh=mesh, in_specs=in_specs, out_specs=out_specs, check_vma=False)
```

```python
import functools

import jax
import jax.numpy as jnp
from jax import lax
from jax.experimental import pallas as pl
from jax.experimental.pallas import tpu as pltpu
from jax.sharding import PartitionSpec as P

MESH = {"occ": 4, "vir": 8}
STEP = 256


def contract_block(left, piece):
    return lax.dot_general(
        left,
        piece,
        (((2,), (2,)), ((0,), (0,))),
        precision=lax.Precision.HIGHEST,
        preferred_element_type=jnp.float32,
    )


def gather_body(amplitudes, integrals):
    gathered = lax.all_gather(amplitudes, "vir", axis=2, tiled=True)
    panel_sum = contract_block(gathered, lax.all_gather(integrals, "occ", axis=2, tiled=True))
    return 0.5 * panel_sum


BOTH = ("occ", "vir")
X, Y = 1, 2


def pairs(move):
    return [(o * 8 + v, move(o, v >> 1, v & 1)) for o in range(4) for v in range(8)]


SAME_CORE = pairs(lambda o, z, c: (o ^ (X if c else Y)) * 8 + 2 * z + c)
CROSS_CORE = pairs(lambda o, z, c: (o ^ (Y if c else X)) * 8 + 2 * z + 1 - c)
FIRST_Z = pairs(lambda o, z, c: o * 8 + 2 * (z ^ (1 if c else 2)) + c)
SECOND_Z = pairs(lambda o, z, c: o * 8 + 2 * (z ^ (2 if c else 1)) + c)
OVER_CORE = pairs(lambda o, z, c: o * 8 + 2 * z + 1 - c)
FIRST_KIND = pairs(lambda o, z, c: (o ^ (Y if c else X)) * 8 + 2 * z + c)
SECOND_KIND = SAME_CORE

VMEM, HBM = pl.BlockSpec(memory_space=pltpu.VMEM), pl.BlockSpec(memory_space=pl.ANY)


def call(kernel, out_shape, in_specs, out_specs, flops, *args, **more):
    arrays = [*args, *jax.tree.leaves(out_shape)]
    return pl.pallas_call(
        kernel,
        out_shape=out_shape,
        in_specs=in_specs,
        out_specs=out_specs,
        compiler_params=pltpu.CompilerParams(vmem_limit_bytes=16 * 1024 * 1024),
        cost_estimate=pl.CostEstimate(flops=flops, bytes_accessed=4 * sum(a.size for a in arrays), transcendentals=0),
        **more,
    )(*args)


def like(a, *shape):
    return jax.ShapeDtypeStruct(shape, a.dtype)


def position():
    o, v = lax.axis_index("occ"), lax.axis_index("vir")
    return o // 2, lax.rem(o, 2), v // 2, lax.rem(v, 2)


def holds():
    y, x, z, core = position()
    return jnp.where(core == 0, z // 2 == y, lax.rem(z, 2) == x)


def kinds_kernel(spans, whole, *refs):
    *out, sems = refs
    core = position()[3]
    copies = []
    for ref, (order, low, high) in zip(out, spans):
        kind = core if order == 0 else 1 - core
        source = whole.at[pl.ds(2 * kind, 2), pl.ds(low, high - low)]
        copies.append(pltpu.make_async_copy(source, ref, sems.at[len(copies)]))
    for copy in copies:
        copy.start()
    for copy in copies:
        copy.wait()


def kinds(a, *cuts):
    n = a.shape[1]
    spans = [(order, low, high) for order, cut in enumerate(cuts) for low, high in zip((0, *cut), (*cut, n))]
    out = [like(a, 2, high - low, a.shape[2]) for _, low, high in spans]
    sems = pltpu.SemaphoreType.DMA((len(spans),))
    pieces = call(functools.partial(kinds_kernel, spans), out, [HBM], [VMEM] * len(out), 0, a, scratch_shapes=[sems])
    return [[p for p, span in zip(pieces, spans) if span[0] == order] for order in range(2)]


def merge_kernel(first, second, out):
    core = position()[3]
    out[core] = first[...]
    out[1 - core] = second[...]


def merge(first, second):
    return call(merge_kernel, like(first, 2, *first.shape), [VMEM] * 2, VMEM, 0, first, second)


def choose_kernel(held, got, out, *small):
    out[...] = jnp.where(holds(), held[...], got[...])
    for ref in small:
        ref[...] = out[0, 0, : ref.shape[0], :]


def choose(held, got, *small):
    shapes = [like(held, *held.shape)] + [like(held, 8, held.shape[3])] * len(small)
    return call(choose_kernel, shapes, [VMEM] * 2, [VMEM] * len(shapes), 0, held, got)


def gate_kernel(a, small, out):
    del a, small, out


def gate(a, small):
    return call(gate_kernel, like(a, *a.shape), [HBM] * 2, HBM, 0, a, small, input_output_aliases={0: 0})


def split(a):
    high = a.astype(jnp.bfloat16)
    low = (a - high.astype(jnp.float32)).astype(jnp.bfloat16)
    return high, low


def dot3(left, right):
    (lh, ll), (rh, rl) = left, right

    def dot(a, b):
        return lax.dot_general(a, b, (((1,), (1,)), ((), ())), preferred_element_type=jnp.float32)

    return dot(lh, rh) + (dot(lh, rl) + dot(ll, rh))


def partial_kernel(order, near, far, *refs):
    *chunks, out = refs
    y, x, z, core = position()
    kind = core if order == 0 else 1 - core
    in_order = jnp.where(kind == 0, lax.rem(z, 2) == x, z // 2 == y)
    for i in range(2):
        first, second = (jnp.concatenate([a[0, i], a[1, i]], axis=1) for a in (near, far))
        t = split(jnp.concatenate([jnp.where(in_order, first, second), jnp.where(in_order, second, first)], axis=1))
        for low in range(0, out.shape[2], STEP):
            high = min(low + STEP, out.shape[2])
            rows, base = [], 0
            for own, got in zip(chunks[::2], chunks[1::2]):
                start, stop = max(low - base, 0), min(high - base, own.shape[1])
                if start < stop:
                    rows.append(jnp.concatenate([own[i, start:stop, :], got[i, start:stop, :]], axis=1))
                base += own.shape[1]
            out[i, :, low:high] = dot3(t, split(jnp.concatenate(rows, axis=0)))


def partial_sum(order, near, far, own, got):
    n_ij, (n_g, _, n_o), n_ab = near.shape[2], own[0].shape, sum(a.shape[1] for a in own)
    chunks = [a for pair in zip(own, got) for a in pair]
    flops = 12 * n_g * n_ij * n_ab * n_o
    specs = [VMEM] * (2 + len(chunks))
    return call(functools.partial(partial_kernel, order), like(near, n_g, n_ij, n_ab), specs, VMEM, flops, near, far, *chunks)


def finish_kernel(order, kept, came, *refs):
    out, result, sems = refs[-3:]
    core = position()[3]
    kind = core if order == 0 else 1 - core
    copies = []
    for i in range(2):
        result[i] = 0.5 * (kept[i] + came[i])
        copies.append(pltpu.make_async_copy(result.at[i], out.at[2 * kind + i], sems.at[i]))
        copies[-1].start()
    for copy in copies:
        copy.wait()


def finish(order, kept, came, *out):
    n_g, *rest = kept.shape
    return call(
        functools.partial(finish_kernel, order),
        like(kept, 2 * n_g, *rest),
        [VMEM, VMEM] + [HBM] * len(out),
        HBM,
        2 * kept.size,
        kept,
        came,
        *out,
        scratch_shapes=[pltpu.VMEM(kept.shape, jnp.float32), pltpu.SemaphoreType.DMA((2,))],
        input_output_aliases={2: 0} if out else {},
    )


def tie(a, *others):
    return lax.optimization_barrier((a, *others))[0]


def permute(a, perm):
    return lax.ppermute(a, BOTH, perm)


def spread(held, short):
    if short:
        ready, small = choose(held, permute(held, FIRST_Z), 1)
        near = gate(ready, permute(small, OVER_CORE))
        near_other = permute(near, OVER_CORE)
        far = permute(near, SECOND_Z)
    else:
        (near,) = choose(held, permute(held, FIRST_Z))
        ready = near
        near_other = permute(near, OVER_CORE)
        far = permute(tie(near, near_other), SECOND_Z)
    return [[near, far], [near_other, permute(far, OVER_CORE)]], ready


def hybrid_body(amplitudes, integrals):
    (mine,), (give,) = kinds(amplitudes, (), ())
    same, cross = permute(mine, SAME_CORE), permute(give, CROSS_CORE)
    n_ab = integrals.shape[1]
    own = kinds(integrals, (n_ab * 51 // 56,), (n_ab * 19 // 28,))
    send, ready = spread(merge(tie(same, *own[0], *own[1]), cross), True)

    own[1] = [tie(a, ready) for a in own[1]]
    got = [[permute(a, perm) for a in pieces] for pieces, perm in zip(own, (FIRST_KIND, SECOND_KIND))]
    came = []
    for order, perm in enumerate((SECOND_KIND, FIRST_KIND)):
        came.append(permute(partial_sum(order, *send[order], own[order], got[order]), perm))

    keep, _ = spread(tie(merge(mine, permute(tie(give, send[0][0]), OVER_CORE)), send[0][1]), False)
    out = []
    for order in range(2):
        kept = partial_sum(order, *keep[order], own[order], got[order])
        out = [finish(order, kept, came[order], *out)]
    return out[0]


def solution(mesh):
    in_specs = (P(None, "occ", "vir"), P(None, "vir", "occ"))
    out_specs = P(None, "occ", "vir")
    body = hybrid_body if dict(mesh.shape) == MESH else gather_body
    return jax.shard_map(body, mesh=mesh, in_specs=in_specs, out_specs=out_specs, check_vma=False)
```
